768 devices in a mesh: dp: 24 (over z, y_hi), shard: 32 (over y_lo, x, core).
Axes of the slice: x: 4, y: 8 (y_hi: 2, y_lo: 4; y = y_hi * 4 + y_lo), z: 12, core: 2. Of those that a mesh axis runs over, the one named last changes fastest.
Arguments:
- out_grad: bfloat16 [12288, 8192], P('dp', 'shard'), may hold values from -6 to 6
- hidden: bfloat16 [12288, 24, 1024], P('dp', None, 'shard'), may hold values from -0.078125 to 0.078125
- basis: bfloat16 [8192, 1024], P('shard'), may hold values from -0.0625 to 0.0625
- moment: float32 [24576, 1024], P(('dp', 'shard')), may hold values from -3 to 3
- second: float32 [24576, 1024], P(('dp', 'shard')), may hold values from 0.001 to 0.01
Outputs:
- update: bfloat16 [24576, 8192], P('dp', 'shard')
- moment_new: float32 [24576, 1024], P(('dp', 'shard'))
- second_new: float32 [24576, 1024], P(('dp', 'shard'))
The draws below stay inside these ranges and needn't reach their ends.
All inputs are finite; a program needn't handle non-finite values.
Results may differ from the reference program's by a relative error of at most 0.0052.
Values may be sent and summed in bfloat16 or wider, within the bound.
No kernel may reach another device: no remote copies, remote signals or barrier semaphores. Data moves between devices by JAX's collectives and lax.ppermute only.
A program may use at most 64 MiB of HBM per device.

```python
import math
import jax
import jax.numpy as jnp

D = 8192
FFW = 24576
RANK = 1024
STEP = 20
TOKENS = 12288
GROUP = 1024
N_DP = 24


def raised(array, stream_key, source, target, blocks, factor):
    owner, partner = [(jnp.arange(array.shape[axis_at]) // (array.shape[axis_at] // blocks)).reshape([-1 if axis == axis_at else 1 for axis in range(array.ndim)]) for axis_at in (source, target)]
    chosen = jax.random.permutation(stream_key, blocks)[partner]
    strong = (owner == chosen) | (owner == (partner + blocks // 2) % blocks)
    return jnp.where(strong, factor * array, array)


def block_levels(own_key, dims, pieces, least, largest):
    gain = 1.0
    for position, blocks in pieces:
        heights = jax.random.uniform(jax.random.fold_in(jax.random.fold_in(own_key, 6), position), (blocks,), jnp.float32, least / len(pieces), largest / len(pieces))
        gain = gain * jnp.repeat(jnp.exp(heights), dims[position] // blocks).reshape((-1,) + (1,) * (len(dims) - 1 - position))
    return gain


def scatter_about(rng, extent, width, most, cuts=(), held_as=jnp.bfloat16):
    values = jax.random.normal(rng, extent, jnp.float32) * width
    if len(cuts) > 0:
        values = block_levels(rng, extent, cuts, -0.22, 0.18) * values
    return jnp.clip(values, min=-most, max=most).astype(held_as)


def bell_draw_with(own_key, shape, deviation, most, cuts, heavy, dtype=jnp.bfloat16):
    entries = deviation * jax.random.normal(own_key, shape, jnp.float32)
    if cuts:
        entries = entries * block_levels(own_key, shape, cuts, -0.22, 0.18)
    return jnp.clip(raised(entries, jax.random.fold_in(own_key, 3), *heavy), -most, most).astype(dtype)


def setup_inputs(seed: int = 0) -> dict:
    key_of = jax.random.split(jax.random.key(seed), 6)
    out_grad = scatter_about(key_of[0], (TOKENS, D), 1.0, 6.0, ((0, 24), (1, 32)))
    hidden = bell_draw_with(key_of[1], (TOKENS, N_DP, GROUP), TOKENS ** -0.5, 0.078125, ((0, 24), (2, 32)), (0, 1, 24, 2.25))
    basis = scatter_about(key_of[2], (D, RANK), D ** -0.5, 0.0625, ((0, 32),))
    moment = scatter_about(key_of[3], (FFW, RANK), 0.2, 3.0, ((0, 768),), jnp.float32)
    second = jnp.clip(jnp.exp(math.log(0.01) - 2.30258502 * jax.random.uniform(key_of[4], (FFW, RANK), jnp.float32) ** block_levels(key_of[4], (FFW, RANK), ((0, 768),), -0.2, 0.2)), 0.001, 0.01)
    return {"out_grad": out_grad, "hidden": hidden, "basis": basis, "moment": moment, "second": second}


def reference(out_grad, hidden, basis, moment, second):
    projected = jnp.dot(out_grad, basis, preferred_element_type=jnp.float32).astype(jnp.bfloat16)
    flat_hidden = hidden.reshape(TOKENS, FFW)
    lowrank = jnp.dot(flat_hidden.T, projected, preferred_element_type=jnp.float32)
    moment_new = 0.9 * moment + 0.1 * lowrank
    second_new = 0.999 * second + 0.001 * lowrank * lowrank
    first_fix = 1.0 - 0.9 ** STEP
    second_fix = 1.0 - 0.999 ** STEP
    direction = (moment_new / first_fix / (jnp.sqrt(second_new / second_fix) + 1e-08)).astype(jnp.bfloat16)
    update = jnp.dot(direction, basis.T, preferred_element_type=jnp.float32).astype(jnp.bfloat16)
    return (update, moment_new, second_new)
```

```python
import jax
import jax.numpy as jnp
from jax import lax
from jax.sharding import Mesh
from jax.sharding import PartitionSpec as P

STEP = 20
NAMES = ("zh", "zl", "yh", "yl", "x", "c")
SIZES = (4, 3, 2, 4, 4, 2)
BF16 = jnp.bfloat16
F32 = jnp.float32


def swap(array, axis):
    return lax.ppermute(array, axis, [(0, 1), (1, 0)])


def along_z(array, step):
    count = SIZES[0] * SIZES[1]
    return lax.ppermute(array, ("zh", "zl"), [(i, (i + step) % count) for i in range(count)])


def gather(array, axes, count):
    return lax.all_to_all(jnp.broadcast_to(array, (count,) + array.shape), axes, 0, 0)


def scatter_sum(array, axes, count, kept=1):
    rows = array.shape[0] // count
    parts = array.astype(BF16).reshape((count, rows) + array.shape[1:])
    parts = lax.all_to_all(parts, axes, 0, 0).astype(F32)
    if kept == 1:
        return jnp.sum(parts, axis=0)
    return jnp.sum(parts.reshape((count // kept, kept) + parts.shape[1:]), axis=0)


def pick(array, axis, index):
    return lax.dynamic_index_in_dim(array, index, axis, keepdims=False)


def dot(left, right, left_dim, right_dim):
    return lax.dot_general(
        left, right, (((left_dim,), (right_dim,)), ((), ())), preferred_element_type=F32
    )


def per_device(out_grad, hidden, basis, moment, second):
    n_zh, n_zl, n_yh, n_yl, n_x, n_c = SIZES
    zl, c = lax.axis_index("zl"), lax.axis_index("c")
    tokens, groups, cols = hidden.shape
    feats, rank = basis.shape
    half = rank // n_c

    both = lax.all_gather(hidden.transpose(1, 2, 0), "c")

    def half_of(index):
        return dot(out_grad, lax.dynamic_slice_in_dim(basis, index * half, half, 1), 1, 0)

    total = half_of(c) + swap(half_of(1 - c).astype(BF16), "c").astype(F32)
    rows = scatter_sum(total, ("x", "yl"), n_x * n_yl).astype(BF16)
    projected = gather(rows, ("x", "yl"), n_x * n_yl).reshape(tokens, half)

    late, projected = lax.optimization_barrier((basis, projected))
    wide = lax.all_gather(late, ("x", "c"), tiled=True)

    both = both.reshape(n_c, n_zh, n_zl, n_yh, cols, tokens)

    def groups_of(step):
        left = pick(both, 2, (zl + step) % n_zl).transpose(1, 2, 0, 3, 4)
        return dot(left.reshape(-1, tokens), projected, 1, 0)

    up = along_z(groups_of(1).astype(BF16), 1)
    down = along_z(groups_of(2).astype(BF16), -1)
    low = groups_of(0) + up.astype(F32) + down.astype(F32)
    low = scatter_sum(low, ("zh", "yh", "c"), n_zh * n_yh * n_c, n_c)
    lowrank = low.transpose(1, 0, 2).reshape(cols, rank)

    moment_new = 0.9 * moment + 0.1 * lowrank
    second_new = 0.999 * second + 0.001 * lowrank * lowrank
    first_fix = 1.0 - 0.9**STEP
    second_fix = 1.0 - 0.999**STEP
    direction = (moment_new / first_fix / (jnp.sqrt(second_new / second_fix) + 1e-08)).astype(BF16)

    rows = gather(direction, "yl", n_yl).reshape(n_yl * cols, rank)
    update = dot(rows, wide, 1, 1).astype(BF16).reshape(n_yl * cols, n_x * n_c, feats)
    update = lax.all_to_all(update.transpose(1, 0, 2), ("x", "c"), 0, 0)
    update = update.reshape(n_x * n_c, n_yl, cols, feats).transpose(1, 0, 2, 3)
    return (update.reshape(-1, feats), moment_new, second_new)


def solution(mesh):
    fine = Mesh(mesh.devices.reshape(SIZES), NAMES)
    dp, shard = NAMES[:3], NAMES[3:]
    every = P(NAMES, None)
    return jax.shard_map(
        per_device,
        mesh=fine,
        in_specs=(P(dp, shard), P(dp, None, shard), P(shard, None), every, every),
        out_specs=(P(dp, shard), every, every),
        check_vma=False,
    )
```

```python
import functools

import jax
import jax.numpy as jnp
from jax import lax
from jax.experimental import pallas as pl
from jax.experimental.pallas import tpu as pltpu
from jax.sharding import Mesh
from jax.sharding import PartitionSpec as P

STEP = 20
NAMES = ("zh", "zl", "yh", "yl", "x", "c")
SIZES = (4, 3, 2, 4, 4, 2)
BF16 = jnp.bfloat16
F32 = jnp.float32


def swap(array, axis):
    return lax.ppermute(array, axis, [(0, 1), (1, 0)])


def along_z(array, step):
    count = SIZES[0] * SIZES[1]
    return lax.ppermute(array, ("zh", "zl"), [(i, (i + step) % count) for i in range(count)])


def gather(array, axes, count):
    return lax.all_to_all(jnp.broadcast_to(array, (count,) + array.shape), axes, 0, 0)


def scatter_sum(array, axes, count, kept=1):
    rows = array.shape[0] // count
    parts = array.astype(BF16).reshape((count, rows) + array.shape[1:])
    parts = lax.all_to_all(parts, axes, 0, 0).astype(F32)
    if kept == 1:
        return jnp.sum(parts, axis=0)
    return jnp.sum(parts.reshape((count // kept, kept) + parts.shape[1:]), axis=0)


def pick(array, axis, index):
    return lax.dynamic_index_in_dim(array, index, axis, keepdims=False)


def dot(left, right, left_dim, right_dim):
    return lax.dot_general(
        left, right, (((left_dim,), (right_dim,)), ((), ())), preferred_element_type=F32
    )


def across(array, axis, count, flip):
    return lax.ppermute(array, axis, [(i, i ^ flip) for i in range(count)])


def products_kernel(n_x, place, rows, *refs):
    *weights, out = refs
    n_c = len(weights) // n_x
    for near in range(n_c):
        for flip in range(n_x):
            index = (place[0] ^ flip) * n_c + (place[1] ^ near)
            out[index] = dot(rows[...], weights[near * n_x + flip][...], 1, 1).astype(BF16)


def products(place, rows, weights):
    feats = weights[0].shape[0]
    vmem = pl.BlockSpec(memory_space=pltpu.VMEM)
    return pl.pallas_call(
        functools.partial(products_kernel, SIZES[4]),
        out_shape=jax.ShapeDtypeStruct((len(weights), rows.shape[0], feats), BF16),
        in_specs=[pl.BlockSpec(memory_space=pltpu.SMEM)] + [vmem] * (1 + len(weights)),
        out_specs=vmem,
        compiler_params=pltpu.CompilerParams(vmem_limit_bytes=16 * 2**20),
        cost_estimate=pl.CostEstimate(
            flops=2 * rows.size * feats * len(weights),
            bytes_accessed=2 * (rows.size + (weights[0].size + rows.shape[0] * feats) * len(weights)),
            transcendentals=0,
        ),
    )(place, rows, *weights)


def per_device(out_grad, hidden, basis, moment, second):
    n_zh, n_zl, n_yh, n_yl, n_x, n_c = SIZES
    zl, x, c = lax.axis_index("zl"), lax.axis_index("x"), lax.axis_index("c")
    tokens, groups, cols = hidden.shape
    feats, rank = basis.shape
    half = rank // n_c

    mine = hidden.transpose(1, 2, 0)
    theirs = swap(mine, "c")

    def half_of(index):
        return dot(out_grad, lax.dynamic_slice_in_dim(basis, index * half, half, 1), 1, 0)

    total = half_of(c) + swap(half_of(1 - c).astype(BF16), "c").astype(F32)
    rows = scatter_sum(total, ("x", "yl"), n_x * n_yl).astype(BF16)
    projected = gather(rows, ("x", "yl"), n_x * n_yl).reshape(tokens, half)

    late, projected = lax.optimization_barrier((basis, projected))
    near = [late] + [across(late, "x", n_x, flip) for flip in range(1, n_x)]

    both = jnp.stack([jnp.where(c == 0, mine, theirs), jnp.where(c == 0, theirs, mine)])
    both = both.reshape(n_c, n_zh, n_zl, n_yh, cols, tokens)

    def groups_of(step):
        left = pick(both, 2, (zl + step) % n_zl).transpose(1, 2, 0, 3, 4)
        return dot(left.reshape(-1, tokens), projected, 1, 0)

    up = along_z(groups_of(1).astype(BF16), 1)
    down = along_z(groups_of(2).astype(BF16), -1)
    low = groups_of(0) + up.astype(F32) + down.astype(F32)
    low, near[1], near[3] = lax.optimization_barrier((low, near[1], near[3]))
    far = [swap(part, "c") for part in near]
    low = scatter_sum(low, ("zh", "yh", "c"), n_zh * n_yh * n_c, n_c)
    lowrank = low.transpose(1, 0, 2).reshape(cols, rank)

    moment_new = 0.9 * moment + 0.1 * lowrank
    second_new = 0.999 * second + 0.001 * lowrank * lowrank
    first_fix = 1.0 - 0.9**STEP
    second_fix = 1.0 - 0.999**STEP
    direction = (moment_new / first_fix / (jnp.sqrt(second_new / second_fix) + 1e-08)).astype(BF16)

    rows = gather(direction, "yl", n_yl).reshape(n_yl * cols, rank)
    update = products(jnp.stack([x, c]).astype(jnp.int32), rows, near + far)
    update = lax.all_to_all(update.reshape(n_x * n_c, n_yl * cols, feats), ("x", "c"), 0, 0)
    update = update.reshape(n_x * n_c, n_yl, cols, feats).transpose(1, 0, 2, 3)
    return (update.reshape(-1, feats), moment_new, second_new)


def solution(mesh):
    fine = Mesh(mesh.devices.reshape(SIZES), NAMES)
    dp, shard = NAMES[:3], NAMES[3:]
    every = P(NAMES, None)
    return jax.shard_map(
        per_device,
        mesh=fine,
        in_specs=(P(dp, shard), P(dp, None, shard), P(shard, None), every, every),
        out_specs=(P(dp, shard), every, every),
        check_vma=False,
    )
```

```python
import functools

import jax
import jax.numpy as jnp
from jax import lax
from jax.experimental import pallas as pl
from jax.experimental.pallas import tpu as pltpu
from jax.sharding import Mesh
from jax.sharding import PartitionSpec as P

STEP = 20
NAMES = ("zh", "zl", "yh", "yl", "x", "c")
SIZES = (4, 3, 2, 4, 4, 2)
BF16 = jnp.bfloat16
F32 = jnp.float32


def swap(array, axis):
    return lax.ppermute(array, axis, [(0, 1), (1, 0)])


def along_z(array, step):
    count = SIZES[0] * SIZES[1]
    return lax.ppermute(array, ("zh", "zl"), [(i, (i + step) % count) for i in range(count)])


def gather(array, axes, count):
    return lax.all_to_all(jnp.broadcast_to(array, (count,) + array.shape), axes, 0, 0)


def scatter_sum(array, axes, count, kept=1):
    rows = array.shape[0] // count
    parts = array.astype(BF16).reshape((count, rows) + array.shape[1:])
    parts = lax.all_to_all(parts, axes, 0, 0).astype(F32)
    if kept == 1:
        return jnp.sum(parts, axis=0)
    return jnp.sum(parts.reshape((count // kept, kept) + parts.shape[1:]), axis=0)


def pick(array, axis, index):
    return lax.dynamic_index_in_dim(array, index, axis, keepdims=False)


def dot(left, right, left_dim, right_dim):
    return lax.dot_general(
        left, right, (((left_dim,), (right_dim,)), ((), ())), preferred_element_type=F32
    )


def across(array, axis, count, flip):
    return lax.ppermute(array, axis, [(i, i ^ flip) for i in range(count)])


def products_kernel(parts, place, own, other, *refs):
    *weights, out = refs
    for flip, count in enumerate(parts):
        at = 0
        for _ in range(count):
            weight = weights.pop(0)
            feats = slice(at, at + weight.shape[0])
            at = feats.stop
            for far, rows in enumerate((own, other)):
                product = dot(rows[...], weight[...], 1, 1)
                out[place[0] ^ flip, place[1] ^ far, :, feats] = product.astype(BF16)


def products(place, own, other, weights):
    rows, feats = own.shape[0], weights[0][0].shape[0]
    parts = [len(group) for group in weights]
    vmem = pl.BlockSpec(memory_space=pltpu.VMEM)
    return pl.pallas_call(
        functools.partial(products_kernel, parts),
        out_shape=jax.ShapeDtypeStruct((len(parts), 2, rows, feats), BF16),
        in_specs=[pl.BlockSpec(memory_space=pltpu.SMEM)] + [vmem] * (2 + sum(parts)),
        out_specs=vmem,
        compiler_params=pltpu.CompilerParams(vmem_limit_bytes=16 * 2**20),
        cost_estimate=pl.CostEstimate(
            flops=4 * own.size * feats * len(parts),
            bytes_accessed=2 * (2 * own.size + feats * (own.shape[1] + 2 * rows) * len(parts)),
            transcendentals=0,
        ),
    )(place, own, other, *sum(weights, []))


def per_device(out_grad, hidden, basis, moment, second):
    n_zh, n_zl, n_yh, n_yl, n_x, n_c = SIZES
    zl, x, c = lax.axis_index("zl"), lax.axis_index("x"), lax.axis_index("c")
    tokens, groups, cols = hidden.shape
    feats, rank = basis.shape
    half = rank // n_c

    mine = hidden.transpose(1, 2, 0)
    theirs = swap(mine, "c")

    def half_of(index):
        return dot(out_grad, lax.dynamic_slice_in_dim(basis, index * half, half, 1), 1, 0)

    total = half_of(c) + swap(half_of(1 - c).astype(BF16), "c").astype(F32)
    rows = scatter_sum(total, ("x", "yl"), n_x * n_yl).astype(BF16)
    projected = gather(rows, ("x", "yl"), n_x * n_yl).reshape(tokens, half)

    late, projected = lax.optimization_barrier((basis, projected))
    near = [[late]] + [[across(late, "x", n_x, flip)] for flip in range(1, n_x - 1)]
    near.append([across(part, "x", n_x, n_x - 1) for part in jnp.split(late, 2)])

    both = jnp.stack([jnp.where(c == 0, mine, theirs), jnp.where(c == 0, theirs, mine)])
    both = both.reshape(n_c, n_zh, n_zl, n_yh, cols, tokens)

    def groups_of(step):
        left = pick(both, 2, (zl + step) % n_zl).transpose(1, 2, 0, 3, 4)
        return dot(left.reshape(-1, tokens), projected, 1, 0)

    up = along_z(groups_of(1).astype(BF16), 1)
    down = along_z(groups_of(2).astype(BF16), -1)
    low = groups_of(0) + up.astype(F32) + down.astype(F32)
    low, near[1][0], near[-1][0] = lax.optimization_barrier((low, near[1][0], near[-1][0]))
    low = scatter_sum(low, ("zh", "yh", "c"), n_zh * n_yh * n_c, n_c)
    lowrank = low.transpose(1, 0, 2).reshape(cols, rank)

    moment_new = 0.9 * moment + 0.1 * lowrank
    second_new = 0.999 * second + 0.001 * lowrank * lowrank
    first_fix = 1.0 - 0.9**STEP
    second_fix = 1.0 - 0.999**STEP
    direction = (moment_new / first_fix / (jnp.sqrt(second_new / second_fix) + 1e-08)).astype(BF16)

    direction, near[1:] = lax.optimization_barrier((direction, near[1:]))

    rows = gather(direction, "yl", n_yl).reshape(n_yl * cols, rank)
    update = products(jnp.stack([x, c]).astype(jnp.int32), rows, swap(rows, "c"), near)
    update = lax.all_to_all(update, "x", 0, 0)
    update = update.reshape(n_x * n_c, n_yl, cols, feats).transpose(1, 0, 2, 3)
    return (update.reshape(-1, feats), moment_new, second_new)


def solution(mesh):
    fine = Mesh(mesh.devices.reshape(SIZES), NAMES)
    dp, shard = NAMES[:3], NAMES[3:]
    every = P(NAMES, None)
    return jax.shard_map(
        per_device,
        mesh=fine,
        in_specs=(P(dp, shard), P(dp, None, shard), P(shard, None), every, every),
        out_specs=(P(dp, shard), every, every),
        check_vma=False,
    )
```

```python
import functools

import jax
import jax.numpy as jnp
from jax import lax
from jax.experimental import pallas as pl
from jax.experimental.pallas import tpu as pltpu
from jax.sharding import Mesh
from jax.sharding import PartitionSpec as P

STEP = 20
NAMES = ("zh", "zl", "yh", "yl", "x", "c")
SIZES = (4, 3, 2, 4, 4, 2)
BF16 = jnp.bfloat16
F32 = jnp.float32


def swap(array, axis):
    return lax.ppermute(array, axis, [(0, 1), (1, 0)])


def along_z(array, step):
    count = SIZES[0] * SIZES[1]
    return lax.ppermute(array, ("zh", "zl"), [(i, (i + step) % count) for i in range(count)])


def gather(array, axes, count):
    return lax.all_to_all(jnp.broadcast_to(array, (count,) + array.shape), axes, 0, 0)


def scatter_sum(array, axes, count, kept=1):
    rows = array.shape[0] // count
    parts = array.astype(BF16).reshape((count, rows) + array.shape[1:])
    parts = lax.all_to_all(parts, axes, 0, 0).astype(F32)
    if kept == 1:
        return jnp.sum(parts, axis=0)
    return jnp.sum(parts.reshape((count // kept, kept) + parts.shape[1:]), axis=0)


def pick(array, axis, index):
    return lax.dynamic_index_in_dim(array, index, axis, keepdims=False)


def dot(left, right, left_dim, right_dim):
    return lax.dot_general(
        left, right, (((left_dim,), (right_dim,)), ((), ())), preferred_element_type=F32
    )


def across(array, axis, count, flip):
    return lax.ppermute(array, axis, [(i, i ^ flip) for i in range(count)])


def products_kernel(parts, place, own, other, *refs):
    *weights, out, full = refs
    half = own.shape[-1]
    count = full.shape[1]
    for core in range(2):
        @pl.when(place[1] == core)
        def _(core=core):
            for far in range(2):
                full[far, :, core * half : (core + 1) * half] = own[:, far].reshape(count, half)
                full[far, :, (1 - core) * half : (2 - core) * half] = other[:, 1 - far].reshape(
                    count, half
                )

    for flip, number in enumerate(parts):
        at = 0
        for _ in range(number):
            weight = weights.pop(0)
            feats = slice(at, at + weight.shape[0])
            at = feats.stop
            for far in range(2):
                product = dot(full[far], weight[...], 1, 1)
                out[place[0] ^ flip, place[1] ^ far, :, feats] = product.astype(BF16)


def products(place, own, other, weights):
    n_yl, _, cols, half = own.shape
    rows, (feats, rank) = n_yl * cols, weights[0][0].shape
    parts = [len(group) for group in weights]
    vmem = pl.BlockSpec(memory_space=pltpu.VMEM)
    return pl.pallas_call(
        functools.partial(products_kernel, parts),
        out_shape=jax.ShapeDtypeStruct((len(parts), 2, rows, feats), BF16),
        in_specs=[pl.BlockSpec(memory_space=pltpu.SMEM)] + [vmem] * (2 + sum(parts)),
        out_specs=vmem,
        scratch_shapes=[pltpu.VMEM((2, rows, rank), BF16)],
        compiler_params=pltpu.CompilerParams(vmem_limit_bytes=16 * 2**20),
        cost_estimate=pl.CostEstimate(
            flops=4 * rows * rank * feats * len(parts),
            bytes_accessed=2 * (2 * rows * rank + feats * (rank + 2 * rows) * len(parts)),
            transcendentals=0,
        ),
    )(place, own, other, *sum(weights, []))


def per_device(out_grad, hidden, basis, moment, second):
    n_zh, n_zl, n_yh, n_yl, n_x, n_c = SIZES
    zl, x, c = lax.axis_index("zl"), lax.axis_index("x"), lax.axis_index("c")
    tokens, groups, cols = hidden.shape
    feats, rank = basis.shape
    half = rank // n_c

    mine = hidden.transpose(1, 2, 0)
    theirs = swap(mine, "c")

    def half_of(index):
        return dot(out_grad, lax.dynamic_slice_in_dim(basis, index * half, half, 1), 1, 0)

    total = half_of(c) + swap(half_of(1 - c).astype(BF16), "c").astype(F32)
    rows = scatter_sum(total, ("x", "yl"), n_x * n_yl).astype(BF16)
    projected = gather(rows, ("x", "yl"), n_x * n_yl).reshape(tokens, half)

    late, projected = lax.optimization_barrier((basis, projected))
    near = [[late]] + [[across(late, "x", n_x, flip)] for flip in range(1, n_x - 1)]
    near.append([across(part, "x", n_x, n_x - 1) for part in jnp.split(late, 2)])

    both = jnp.stack([mine, theirs]).reshape(n_c, n_zh, n_zl, n_yh, cols, tokens)

    def part(array, index):
        return lax.dynamic_slice_in_dim(array, index * half, half, 1)

    kept = jnp.stack([part(moment, c), part(second, c)])
    moments = jnp.stack([kept, swap(jnp.stack([part(moment, 1 - c), part(second, 1 - c)]), "c")], axis=1)

    def groups_of(step):
        left = pick(both, 2, (zl + step) % n_zl).transpose(1, 2, 0, 3, 4)
        return dot(left.reshape(-1, tokens), projected, 1, 0)

    up = along_z(groups_of(1).astype(BF16), 1)
    down = along_z(groups_of(2).astype(BF16), -1)
    low = groups_of(0) + up.astype(F32) + down.astype(F32)
    low, near[1][0], near[-1][0] = lax.optimization_barrier((low, near[1][0], near[-1][0]))
    low = scatter_sum(low, ("zh", "yh"), n_zh * n_yh)
    lowrank = low.reshape(n_c, cols, half)

    moment_new = 0.9 * moments[0] + 0.1 * lowrank
    second_new = 0.999 * moments[1] + 0.001 * lowrank * lowrank
    first_fix = 1.0 - 0.9**STEP
    second_fix = 1.0 - 0.999**STEP
    direction = (moment_new / first_fix / (jnp.sqrt(second_new / second_fix) + 1e-08)).astype(BF16)

    direction, near[1:] = lax.optimization_barrier((direction, near[1:]))

    rows = gather(direction, "yl", n_yl)
    back = swap(jnp.stack([moment_new[1], second_new[1]]), "c")

    def whole(own, other):
        return jnp.concatenate(
            [jnp.where(c == 0, own, other), jnp.where(c == 0, other, own)], axis=1
        )

    update = products(jnp.stack([x, c]).astype(jnp.int32), rows, swap(rows, "c"), near)
    update = lax.all_to_all(update, "x", 0, 0)
    update = update.reshape(n_x * n_c, n_yl, cols, feats).transpose(1, 0, 2, 3)
    return (
        update.reshape(-1, feats),
        whole(moment_new[0], back[0]),
        whole(second_new[0], back[1]),
    )


def solution(mesh):
    fine = Mesh(mesh.devices.reshape(SIZES), NAMES)
    dp, shard = NAMES[:3], NAMES[3:]
    every = P(NAMES, None)
    return jax.shard_map(
        per_device,
        mesh=fine,
        in_specs=(P(dp, shard), P(dp, None, shard), P(shard, None), every, every),
        out_specs=(P(dp, shard), every, every),
        check_vma=False,
    )
```

```python
import functools

import jax
import jax.numpy as jnp
from jax import lax
from jax.experimental import pallas as pl
from jax.experimental.pallas import tpu as pltpu
from jax.sharding import Mesh
from jax.sharding import PartitionSpec as P

STEP = 20
NAMES = ("zh", "zl", "yh", "yl", "x", "c")
SIZES = (4, 3, 2, 4, 4, 2)
BF16 = jnp.bfloat16
F32 = jnp.float32


def swap(array, axis):
    return lax.ppermute(array, axis, [(0, 1), (1, 0)])


def along_z(array, step):
    count = SIZES[0] * SIZES[1]
    return lax.ppermute(array, ("zh", "zl"), [(i, (i + step) % count) for i in range(count)])


def gather(array, axes, count):
    return lax.all_to_all(jnp.broadcast_to(array, (count,) + array.shape), axes, 0, 0)


def scatter_sum(array, axes, count, kept=1):
    rows = array.shape[0] // count
    parts = array.astype(BF16).reshape((count, rows) + array.shape[1:])
    parts = lax.all_to_all(parts, axes, 0, 0).astype(F32)
    if kept == 1:
        return jnp.sum(parts, axis=0)
    return jnp.sum(parts.reshape((count // kept, kept) + parts.shape[1:]), axis=0)


def pick(array, axis, index):
    return lax.dynamic_index_in_dim(array, index, axis, keepdims=False)


def dot(left, right, left_dim, right_dim):
    return lax.dot_general(
        left, right, (((left_dim,), (right_dim,)), ((), ())), preferred_element_type=F32
    )


def across(array, axis, count, flip):
    return lax.ppermute(array, axis, [(i, i ^ flip) for i in range(count)])


def products_kernel(parts, place, own, other, *refs):
    *weights, out, full = refs
    half = own.shape[-1]
    count = full.shape[0] // 2
    for core in range(2):
        @pl.when(place[1] == core)
        def _(core=core):
            for far in range(2):
                rows = slice(far * count, (far + 1) * count)
                full[rows, core * half : (core + 1) * half] = own[:, far].reshape(count, half)
                full[rows, (1 - core) * half : (2 - core) * half] = other[:, 1 - far].reshape(
                    count, half
                )

    for flip, number in enumerate(parts):
        at = 0
        for _ in range(number):
            weight = weights.pop(0)
            feats = slice(at, at + weight.shape[0])
            at = feats.stop
            product = dot(full[...], weight[...], 1, 1).astype(BF16)
            for far in range(2):
                rows = slice(far * count, (far + 1) * count)
                out[place[0] ^ flip, place[1] ^ far, :, feats] = product[rows]


def products(place, own, other, weights):
    n_yl, _, cols, half = own.shape
    rows, (feats, rank) = n_yl * cols, weights[0][0].shape
    parts = [len(group) for group in weights]
    vmem = pl.BlockSpec(memory_space=pltpu.VMEM)
    return pl.pallas_call(
        functools.partial(products_kernel, parts),
        out_shape=jax.ShapeDtypeStruct((len(parts), 2, rows, feats), BF16),
        in_specs=[pl.BlockSpec(memory_space=pltpu.SMEM)] + [vmem] * (2 + sum(parts)),
        out_specs=vmem,
        scratch_shapes=[pltpu.VMEM((2 * rows, rank), BF16)],
        compiler_params=pltpu.CompilerParams(vmem_limit_bytes=16 * 2**20),
        cost_estimate=pl.CostEstimate(
            flops=4 * rows * rank * feats * len(parts),
            bytes_accessed=2 * (2 * rows * rank + feats * (rank + 2 * rows) * len(parts)),
            transcendentals=0,
        ),
    )(place, own, other, *sum(weights, []))


def per_device(out_grad, hidden, basis, moment, second):
    n_zh, n_zl, n_yh, n_yl, n_x, n_c = SIZES
    zl, x, c = lax.axis_index("zl"), lax.axis_index("x"), lax.axis_index("c")
    tokens, groups, cols = hidden.shape
    feats, rank = basis.shape
    half = rank // n_c

    mine = hidden.transpose(1, 2, 0)
    theirs = swap(mine, "c")

    def half_of(index):
        return dot(out_grad, lax.dynamic_slice_in_dim(basis, index * half, half, 1), 1, 0)

    total = half_of(c) + swap(half_of(1 - c).astype(BF16), "c").astype(F32)
    rows = scatter_sum(total, ("x", "yl"), n_x * n_yl).astype(BF16)
    projected = gather(rows, ("x", "yl"), n_x * n_yl).reshape(tokens, half)

    late, projected = lax.optimization_barrier((basis, projected))
    near = [[late]] + [[across(late, "x", n_x, flip)] for flip in range(1, n_x - 1)]
    near.append([across(part, "x", n_x, n_x - 1) for part in jnp.split(late, 2)])

    both = jnp.stack([mine, theirs]).reshape(n_c, n_zh, n_zl, n_yh, cols, tokens)

    def part(array, index):
        return lax.dynamic_slice_in_dim(array, index * half, half, 1)

    kept = jnp.stack([part(moment, c), part(second, c)])
    moments = jnp.stack([kept, swap(jnp.stack([part(moment, 1 - c), part(second, 1 - c)]), "c")], axis=1)

    def groups_of(step):
        left = pick(both, 2, (zl + step) % n_zl).transpose(1, 2, 0, 3, 4)
        return dot(left.reshape(-1, tokens), projected, 1, 0)

    up = along_z(groups_of(1).astype(BF16), 1)
    down = along_z(groups_of(2).astype(BF16), -1)
    low = groups_of(0) + up.astype(F32) + down.astype(F32)
    low, near[1][0], near[-1][0] = lax.optimization_barrier((low, near[1][0], near[-1][0]))
    low = scatter_sum(low, ("zh", "yh"), n_zh * n_yh)
    lowrank = low.reshape(n_c, cols, half)

    moment_new = 0.9 * moments[0] + 0.1 * lowrank
    second_new = 0.999 * moments[1] + 0.001 * lowrank * lowrank
    first_fix = 1.0 - 0.9**STEP
    second_fix = 1.0 - 0.999**STEP
    direction = (moment_new / first_fix / (jnp.sqrt(second_new / second_fix) + 1e-08)).astype(BF16)

    direction, near[1:] = lax.optimization_barrier((direction, near[1:]))

    rows = gather(direction, "yl", n_yl)
    back = swap(jnp.stack([moment_new[1], second_new[1]]), "c")

    def whole(own, other):
        return jnp.concatenate(
            [jnp.where(c == 0, own, other), jnp.where(c == 0, other, own)], axis=1
        )

    update = products(jnp.stack([x, c]).astype(jnp.int32), rows, swap(rows, "c"), near)
    update = lax.all_to_all(update, "x", 0, 0)
    update = update.reshape(n_x * n_c, n_yl, cols, feats).transpose(1, 0, 2, 3)
    return (
        update.reshape(-1, feats),
        whole(moment_new[0], back[0]),
        whole(second_new[0], back[1]),
    )


def solution(mesh):
    fine = Mesh(mesh.devices.reshape(SIZES), NAMES)
    dp, shard = NAMES[:3], NAMES[3:]
    every = P(NAMES, None)
    return jax.shard_map(
        per_device,
        mesh=fine,
        in_specs=(P(dp, shard), P(dp, None, shard), P(shard, None), every, every),
        out_specs=(P(dp, shard), every, every),
        check_vma=False,
    )
```

```python
import functools

import jax
import jax.numpy as jnp
from jax import lax
from jax.experimental import pallas as pl
from jax.experimental.pallas import tpu as pltpu
from jax.sharding import Mesh
from jax.sharding import PartitionSpec as P

STEP = 20
NAMES = ("zh", "zl", "yh", "yl", "x", "c")
SIZES = (4, 3, 2, 4, 4, 2)
BF16 = jnp.bfloat16
F32 = jnp.float32


def swap(array, axis):
    return lax.ppermute(array, axis, [(0, 1), (1, 0)])


def along_z(array, step):
    count = SIZES[0] * SIZES[1]
    return lax.ppermute(array, ("zh", "zl"), [(i, (i + step) % count) for i in range(count)])


def gather(array, axes, count):
    return lax.all_to_all(jnp.broadcast_to(array, (count,) + array.shape), axes, 0, 0)


def scatter_sum(array, axes, count, kept=1):
    rows = array.shape[0] // count
    parts = array.astype(BF16).reshape((count, rows) + array.shape[1:])
    parts = lax.all_to_all(parts, axes, 0, 0).astype(F32)
    if kept == 1:
        return jnp.sum(parts, axis=0)
    return jnp.sum(parts.reshape((count // kept, kept) + parts.shape[1:]), axis=0)


def pick(array, axis, index):
    return lax.dynamic_index_in_dim(array, index, axis, keepdims=False)


def dot(left, right, left_dim, right_dim):
    return lax.dot_general(
        left, right, (((left_dim,), (right_dim,)), ((), ())), preferred_element_type=F32
    )


def across(array, axis, count, flip):
    return lax.ppermute(array, axis, [(i, i ^ flip) for i in range(count)])


def products_kernel(parts, place, own, other, *refs):
    *weights, out, full = refs
    half = own.shape[-1]
    count = full.shape[0] // 2
    for core in range(2):
        @pl.when(place[1] == core)
        def _(core=core):
            for far in range(2):
                rows = slice(far * count, (far + 1) * count)
                full[rows, core * half : (core + 1) * half] = own[:, far].reshape(count, half)
                full[rows, (1 - core) * half : (2 - core) * half] = other[:, 1 - far].reshape(
                    count, half
                )

    for flip, number in enumerate(parts):
        at = 0
        for _ in range(number):
            weight = weights.pop(0)
            feats = slice(at, at + weight.shape[0])
            at = feats.stop
            product = dot(full[...], weight[...], 1, 1).astype(BF16)
            for far in range(2):
                rows = slice(far * count, (far + 1) * count)
                out[place[0] ^ flip, place[1] ^ far, :, feats] = product[rows]


def products(place, own, other, weights):
    n_yl, _, cols, half = own.shape
    rows, (feats, rank) = n_yl * cols, weights[0][0].shape
    parts = [len(group) for group in weights]
    vmem = pl.BlockSpec(memory_space=pltpu.VMEM)
    return pl.pallas_call(
        functools.partial(products_kernel, parts),
        out_shape=jax.ShapeDtypeStruct((len(parts), 2, rows, feats), BF16),
        in_specs=[pl.BlockSpec(memory_space=pltpu.SMEM)] + [vmem] * (2 + sum(parts)),
        out_specs=vmem,
        scratch_shapes=[pltpu.VMEM((2 * rows, rank), BF16)],
        compiler_params=pltpu.CompilerParams(vmem_limit_bytes=16 * 2**20),
        cost_estimate=pl.CostEstimate(
            flops=4 * rows * rank * feats * len(parts),
            bytes_accessed=2 * (2 * rows * rank + feats * (rank + 2 * rows) * len(parts)),
            transcendentals=0,
        ),
    )(place, own, other, *sum(weights, []))


def per_device(out_grad, hidden, basis, moment, second):
    n_zh, n_zl, n_yh, n_yl, n_x, n_c = SIZES
    zl, x, c = lax.axis_index("zl"), lax.axis_index("x"), lax.axis_index("c")
    tokens, groups, cols = hidden.shape
    feats, rank = basis.shape
    half = rank // n_c

    mine = hidden.transpose(1, 2, 0)
    theirs = swap(mine, "c")

    def half_of(index):
        return dot(out_grad, lax.dynamic_slice_in_dim(basis, index * half, half, 1), 1, 0)

    total = half_of(c) + swap(half_of(1 - c).astype(BF16), "c").astype(F32)
    rows = scatter_sum(total, ("x", "yl"), n_x * n_yl).astype(BF16)
    projected = gather(rows, ("x", "yl"), n_x * n_yl).reshape(tokens, half)

    late, projected = lax.optimization_barrier((basis, projected))
    near = [[late]] + [[across(late, "x", n_x, flip)] for flip in range(1, n_x - 1)]
    near.append([across(part, "x", n_x, n_x - 1) for part in jnp.split(late, [3 * late.shape[0] // 4])])

    both = jnp.stack([mine, theirs]).reshape(n_c, n_zh, n_zl, n_yh, cols, tokens)

    def part(array, index):
        return lax.dynamic_slice_in_dim(array, index * half, half, 1)

    kept = jnp.stack([part(moment, c), part(second, c)])
    moments = jnp.stack([kept, swap(jnp.stack([part(moment, 1 - c), part(second, 1 - c)]), "c")], axis=1)

    def groups_of(step):
        left = pick(both, 2, (zl + step) % n_zl).transpose(1, 2, 0, 3, 4)
        return dot(left.reshape(-1, tokens), projected, 1, 0)

    up = along_z(groups_of(1).astype(BF16), 1)
    down = along_z(groups_of(2).astype(BF16), -1)
    low = groups_of(0) + up.astype(F32) + down.astype(F32)
    low, near[1][0], near[-1][0] = lax.optimization_barrier((low, near[1][0], near[-1][0]))
    low = scatter_sum(low, ("zh", "yh"), n_zh * n_yh)
    lowrank = low.reshape(n_c, cols, half)

    moment_new = 0.9 * moments[0] + 0.1 * lowrank
    second_new = 0.999 * moments[1] + 0.001 * lowrank * lowrank
    first_fix = 1.0 - 0.9**STEP
    second_fix = 1.0 - 0.999**STEP
    direction = (moment_new / first_fix / (jnp.sqrt(second_new / second_fix) + 1e-08)).astype(BF16)

    direction, near[1:] = lax.optimization_barrier((direction, near[1:]))

    rows = gather(direction, "yl", n_yl)
    back = swap(jnp.stack([moment_new[1], second_new[1]]), "c")

    def whole(own, other):
        return jnp.concatenate(
            [jnp.where(c == 0, own, other), jnp.where(c == 0, other, own)], axis=1
        )

    update = products(jnp.stack([x, c]).astype(jnp.int32), rows, swap(rows, "c"), near)
    update = lax.all_to_all(update, "x", 0, 0)
    update = update.reshape(n_x * n_c, n_yl, cols, feats).transpose(1, 0, 2, 3)
    return (
        update.reshape(-1, feats),
        whole(moment_new[0], back[0]),
        whole(second_new[0], back[1]),
    )


def solution(mesh):
    fine = Mesh(mesh.devices.reshape(SIZES), NAMES)
    dp, shard = NAMES[:3], NAMES[3:]
    every = P(NAMES, None)
    return jax.shard_map(
        per_device,
        mesh=fine,
        in_specs=(P(dp, shard), P(dp, None, shard), P(shard, None), every, every),
        out_specs=(P(dp, shard), every, every),
        check_vma=False,
    )
```

```python
import functools

import jax
import jax.numpy as jnp
from jax import lax
from jax.experimental import pallas as pl
from jax.experimental.pallas import tpu as pltpu
from jax.sharding import Mesh
from jax.sharding import PartitionSpec as P

STEP = 20
NAMES = ("zh", "zl", "yh", "yl", "x", "c")
SIZES = (4, 3, 2, 4, 4, 2)
BF16 = jnp.bfloat16
F32 = jnp.float32


def swap(array, axis):
    return lax.ppermute(array, axis, [(0, 1), (1, 0)])


def along_z(array, step):
    count = SIZES[0] * SIZES[1]
    return lax.ppermute(array, ("zh", "zl"), [(i, (i + step) % count) for i in range(count)])


def gather(array, axes, count):
    return lax.all_to_all(jnp.broadcast_to(array, (count,) + array.shape), axes, 0, 0)


def scatter_sum(array, axes, count, kept=1):
    rows = array.shape[0] // count
    parts = array.astype(BF16).reshape((count, rows) + array.shape[1:])
    parts = lax.all_to_all(parts, axes, 0, 0).astype(F32)
    if kept == 1:
        return jnp.sum(parts, axis=0)
    return jnp.sum(parts.reshape((count // kept, kept) + parts.shape[1:]), axis=0)


def pick(array, axis, index):
    return lax.dynamic_index_in_dim(array, index, axis, keepdims=False)


def dot(left, right, left_dim, right_dim):
    return lax.dot_general(
        left, right, (((left_dim,), (right_dim,)), ((), ())), preferred_element_type=F32
    )


def across(array, axis, count, flip):
    return lax.ppermute(array, axis, [(i, i ^ flip) for i in range(count)])


def products_kernel(parts, place, own, other, *refs):
    *weights, out, full = refs
    half = own.shape[-1]
    count = full.shape[0] // 2
    for core in range(2):
        @pl.when(place[1] == core)
        def _(core=core):
            for far in range(2):
                rows = slice(far * count, (far + 1) * count)
                full[rows, core * half : (core + 1) * half] = own[:, far].reshape(count, half)
                full[rows, (1 - core) * half : (2 - core) * half] = other[:, 1 - far].reshape(
                    count, half
                )

    for flip, number in enumerate(parts):
        at = 0
        for _ in range(number):
            weight = weights.pop(0)
            feats = slice(at, at + weight.shape[0])
            at = feats.stop
            product = dot(full[...], weight[...], 1, 1).astype(BF16)
            for far in range(2):
                rows = slice(far * count, (far + 1) * count)
                out[place[0] ^ flip, place[1] ^ far, :, feats] = product[rows]


def products(place, own, other, weights):
    n_yl, _, cols, half = own.shape
    rows, (feats, rank) = n_yl * cols, weights[0][0].shape
    parts = [len(group) for group in weights]
    vmem = pl.BlockSpec(memory_space=pltpu.VMEM)
    return pl.pallas_call(
        functools.partial(products_kernel, parts),
        out_shape=jax.ShapeDtypeStruct((len(parts), 2, rows, feats), BF16),
        in_specs=[pl.BlockSpec(memory_space=pltpu.SMEM)] + [vmem] * (2 + sum(parts)),
        out_specs=vmem,
        scratch_shapes=[pltpu.VMEM((2 * rows, rank), BF16)],
        compiler_params=pltpu.CompilerParams(vmem_limit_bytes=16 * 2**20),
        cost_estimate=pl.CostEstimate(
            flops=4 * rows * rank * feats * len(parts),
            bytes_accessed=2 * (2 * rows * rank + feats * (rank + 2 * rows) * len(parts)),
            transcendentals=0,
        ),
    )(place, own, other, *sum(weights, []))


def per_device(out_grad, hidden, basis, moment, second):
    n_zh, n_zl, n_yh, n_yl, n_x, n_c = SIZES
    zl, x, c = lax.axis_index("zl"), lax.axis_index("x"), lax.axis_index("c")
    tokens, groups, cols = hidden.shape
    feats, rank = basis.shape
    half = rank // n_c

    mine = hidden.transpose(1, 2, 0)
    theirs = swap(mine, "c")

    def half_of(index):
        return dot(out_grad, lax.dynamic_slice_in_dim(basis, index * half, half, 1), 1, 0)

    total = half_of(c) + swap(half_of(1 - c).astype(BF16), "c").astype(F32)
    rows = scatter_sum(total, ("x", "yl"), n_x * n_yl).astype(BF16)
    projected = gather(rows, ("x", "yl"), n_x * n_yl).reshape(tokens, half)

    late, projected = lax.optimization_barrier((basis, projected))
    near = [[late]] + [[across(late, "x", n_x, flip)] for flip in range(1, n_x - 1)]
    near.append([across(part, "x", n_x, n_x - 1) for part in jnp.split(late, [3 * late.shape[0] // 4])])

    both = jnp.stack([mine, theirs]).reshape(n_c, n_zh, n_zl, n_yh, cols, tokens)

    def part(array, index):
        return lax.dynamic_slice_in_dim(array, index * half, half, 1)

    kept = jnp.stack([part(moment, c), part(second, c)])
    moments = jnp.stack([kept, swap(jnp.stack([part(moment, 1 - c), part(second, 1 - c)]), "c")], axis=1)

    def groups_of(step):
        left = pick(both, 2, (zl + step) % n_zl).transpose(1, 2, 0, 3, 4)
        return dot(left.reshape(-1, tokens), projected, 1, 0)

    up = along_z(groups_of(1).astype(BF16), 1)
    down = along_z(groups_of(2).astype(BF16), -1)
    low = groups_of(0) + up.astype(F32) + down.astype(F32)
    low, near[1][0], near[-1][0] = lax.optimization_barrier((low, near[1][0], near[-1][0]))
    low = scatter_sum(low, ("zh", "yh"), n_zh * n_yh)
    lowrank = low.reshape(n_c, cols, half)

    moment_new = 0.9 * moments[0] + 0.1 * lowrank
    second_new = 0.999 * moments[1] + 0.001 * lowrank * lowrank
    first_fix = 1.0 - 0.9**STEP
    second_fix = 1.0 - 0.999**STEP
    direction = (moment_new / first_fix / (jnp.sqrt(second_new / second_fix) + 1e-08)).astype(BF16)

    direction, near[1:] = lax.optimization_barrier((direction, near[1:]))

    rows = gather(direction, "yl", n_yl)
    back = swap(jnp.stack([moment_new[1], second_new[1]]), "c")
    rows, back = lax.optimization_barrier((rows, back))

    def whole(own, other):
        return jnp.concatenate(
            [jnp.where(c == 0, own, other), jnp.where(c == 0, other, own)], axis=1
        )

    update = products(jnp.stack([x, c]).astype(jnp.int32), rows, swap(rows, "c"), near)
    update = lax.all_to_all(update, "x", 0, 0)
    update = update.reshape(n_x * n_c, n_yl, cols, feats).transpose(1, 0, 2, 3)
    return (
        update.reshape(-1, feats),
        whole(moment_new[0], back[0]),
        whole(second_new[0], back[1]),
    )


def solution(mesh):
    fine = Mesh(mesh.devices.reshape(SIZES), NAMES)
    dp, shard = NAMES[:3], NAMES[3:]
    every = P(NAMES, None)
    return jax.shard_map(
        per_device,
        mesh=fine,
        in_specs=(P(dp, shard), P(dp, None, shard), P(shard, None), every, every),
        out_specs=(P(dp, shard), every, every),
        check_vma=False,
    )
```
